32 devices in a mesh: seq: 8 (over z, x), tensor: 4 (over y, core).
Axes of the slice: x: 2, y: 2, z: 4, core: 2. Of those that a mesh axis runs over, the one named last changes fastest.
Arguments:
- queries: bfloat16 [7168, 2048], P('seq', 'tensor'), may hold values from -256 to 256
- db_states: bfloat16 [128, 64, 896], P('seq', None, 'tensor'), may hold values from -4096 to 4096
- enc_gain: float32 [896], replicated, may hold values from 0.1 to 1.9
- kv_weight: bfloat16 [896, 2, 2048], P(None, None, 'tensor'), may hold values from -0.1875 to 0.1875
- shard_ids: int32 [112, 2], P('seq'), may hold values from 0 to 7, as said below
- offsets: int32 [112, 2], P('seq'), may hold values from 0 to 14
Outputs:
- attention_out: bfloat16 [7168, 2048], P('seq', 'tensor')
The draws below stay inside these ranges and needn't reach their ends.
Inputs may be any that keep to these rules, and one draw needn't show every extreme that they name: `shard_ids`: the neighbours named by the 14 groups of one device lie at most 4 in any one shard, and some shard is named exactly 4 times by the groups of every device.
All inputs are finite; a program needn't handle non-finite values.
Results may differ from the reference program's by a relative error of at most 0.0087.
Values may be sent and summed in bfloat16 or wider, within the bound.
A program may use at most 64 MiB of HBM per device.

```python
import math
import jax
import jax.numpy as jnp
from jax import lax

ENC = 896
HEADS = 16
HEAD_DIM = 128
GROUP = 64
CH_DEV = 14
DB_DEV = 16
GROUPS = 112
TOKENS = 7168
N_SEQ = 8


def draw_queries(key, part):
    key = jax.random.fold_in(key, 11)
    key_base = jax.random.fold_in(key, 0)
    shape = (TOKENS, HEADS * HEAD_DIM)
    return jnp.clip(2.0 * jax.random.normal(key_base, shape, jnp.float32), -10.0, 10.0).astype(jnp.bfloat16)


def draw_db_states(key, part):
    key = jax.random.fold_in(key, 23)
    key_base, key_rows, key_cols = jax.random.split(key, 3)
    shape = (DB_DEV * N_SEQ, GROUP, ENC)
    ramp = jnp.arange(ENC, dtype=jnp.float32) / (ENC - 1)
    spread = jnp.exp(jax.random.uniform(key_cols, (ENC,), jnp.float32, 0.0, math.log(10.0)))
    base = jnp.clip(jax.random.normal(key_base, shape, jnp.float32), -4.0, 4.0)
    columns = spread * 3.0 ** ramp
    rows = jnp.exp(jax.random.uniform(key_rows, (DB_DEV * N_SEQ, GROUP, 1), jnp.float32, 0.0, math.log(10.0)))
    return (base * rows * columns).astype(jnp.bfloat16)


def draw_shard_ids(key, part):
    key = jax.random.fold_in(key, 37)
    owners = N_SEQ
    slot_cap = (2 * CH_DEV + N_SEQ - 1) // N_SEQ
    wanted = 2 * CH_DEV
    slot_total = owners * slot_cap
    key_hot, key_pop, key_base, key_order = jax.random.split(key, 4)
    hot_shard = jax.random.randint(key_hot, (), 0, owners)
    popular = jax.random.randint(key_pop, (owners,), 1, 5)
    slot_owner = jnp.arange(slot_total, dtype=jnp.int32) // slot_cap
    base = jax.random.randint(key_base, (owners, slot_total), 0, 4096)
    scores = base * popular[slot_owner][None, :] + jnp.where(slot_owner == hot_shard, 65536, 0)[None, :]
    scores = scores * slot_total + jnp.arange(slot_total, dtype=jnp.int32)[None, :]
    chosen = lax.top_k(scores, wanted)[1]
    shuffle = jax.random.randint(key_order, (owners, wanted), 0, 65536) * wanted + jnp.arange(wanted, dtype=jnp.int32)[None, :]
    order = lax.top_k(shuffle, wanted)[1]
    chosen = jnp.take_along_axis(chosen, order, axis=1)
    return (chosen // slot_cap).reshape(owners * CH_DEV, 2).astype(jnp.int32)


def touch_ends(values, own_key, low, top_value):
    longest = values.shape.index(max(values.shape))
    spots = []
    for shift in (0, 1):
        where = [jax.random.randint(jax.random.fold_in(own_key, axis), (), 0, length) for axis, length in enumerate(values.shape)]
        where[longest] = (where[longest] + shift) % values.shape[longest]
        spots.append(tuple(where))
    return values.at[spots[0]].set(low).at[spots[1]].set(top_value)


def block_levels(rng, shape, pieces, low, top_value):
    def one(position, parts):
        steps = jax.random.uniform(jax.random.fold_in(jax.random.fold_in(rng, 6), position), (parts,), jnp.float32, low / len(pieces), top_value / len(pieces))
        return jnp.repeat(jnp.exp(steps), shape[position] // parts).reshape((-1,) + (1,) * (len(shape) - position - 1))

    gain = one(*pieces[0])
    for cut in pieces[1:]:
        gain = gain * one(*cut)
    return gain


def scatter_about(key, shape, width, limit, cuts=(), kind=jnp.bfloat16):
    level = block_levels(key, shape, cuts, -0.22, 0.18) if cuts else 1.0
    array = jax.random.normal(key, shape, jnp.float32) * width * level
    return jnp.minimum(jnp.maximum(array, -limit), limit).astype(kind)


def setup_inputs(seed: int = 0) -> dict:
    seeds = jax.random.split(jax.random.key(seed), 7)
    return {
        "queries": draw_queries(jax.random.fold_in(seeds[6], 71), 0),
        "db_states": draw_db_states(jax.random.fold_in(seeds[6], 71), 0),
        "enc_gain": jnp.clip(1.0 + 0.18 * jax.random.normal(seeds[2], (ENC,), jnp.float32), 0.1, 1.9),
        "kv_weight": scatter_about(seeds[3], (ENC, 2, HEADS * HEAD_DIM), ENC ** -0.5, 0.1875, ((2, 4),)),
        "shard_ids": draw_shard_ids(jax.random.fold_in(seeds[6], 71), 0),
        "offsets": touch_ends(jax.random.randint(seeds[5], (GROUPS, 2), 0, DB_DEV - 1), jax.random.fold_in(seeds[5], 1), 0, (DB_DEV - 1) - 1).astype(jnp.int32),
    }


epsilon = 1e-06

def attend(query_win, kv_win):
    keys = kv_win[:, :, 0].astype(jnp.float32)
    values = kv_win[:, :, 1].astype(jnp.float32)
    scores = jnp.einsum('wqhd,wkhd->whqk', query_win.astype(jnp.float32), keys) / math.sqrt(HEAD_DIM)
    highest = lax.optimization_barrier(jnp.max(scores, axis=-1, keepdims=True))
    expo = jnp.exp(scores - highest)
    weights = (expo / lax.optimization_barrier(jnp.sum(expo, axis=-1, keepdims=True))).astype(jnp.bfloat16)
    mixed = jnp.einsum('whqk,wkhd->wqhd', weights.astype(jnp.float32), values).astype(jnp.bfloat16)
    return mixed.reshape(query_win.shape[0] * query_win.shape[1], -1)

def reference(queries, db_states, enc_gain, kv_weight, shard_ids, offsets):
    query_cols = HEADS * HEAD_DIM
    projection = kv_weight.reshape(ENC, 2 * query_cols)
    shifted = jnp.concatenate([queries[GROUP - 1:], jnp.zeros((GROUP - 1, query_cols), jnp.bfloat16)], axis=0)
    chosen = (shard_ids * DB_DEV + offsets).astype(jnp.int32)

    def one_block(block):
        ids = lax.dynamic_slice_in_dim(chosen, block * CH_DEV, CH_DEV, 0)
        neigh = jnp.concatenate([db_states[ids], db_states[ids + 1]], axis=2)
        as_float = neigh.astype(jnp.float32)
        inv_rms = lax.rsqrt(lax.optimization_barrier(jnp.mean(as_float * as_float, axis=-1)) + epsilon)
        scaled = (as_float * enc_gain).astype(jnp.bfloat16)
        products = jnp.dot(scaled.reshape(-1, ENC), projection, preferred_element_type=jnp.float32)
        keys_values = (products * inv_rms.reshape(-1, 1)).astype(jnp.bfloat16)
        keys_values = keys_values.reshape(CH_DEV, 4 * GROUP, 2, HEADS, HEAD_DIM)
        window = lax.dynamic_slice_in_dim(shifted, block * CH_DEV * GROUP, CH_DEV * GROUP, 0)
        window = window.reshape(CH_DEV, GROUP, HEADS, HEAD_DIM)
        return attend(window, keys_values)
    blocks = lax.map(one_block, jnp.arange(N_SEQ, dtype=jnp.int32))
    attended = blocks.reshape(TOKENS, query_cols)
    return jnp.concatenate([jnp.zeros((GROUP - 1, query_cols), jnp.bfloat16), attended[:TOKENS - GROUP + 1]], axis=0)
```

```python
import functools
import math

import jax
import jax.numpy as jnp
from jax import lax
from jax.experimental import pallas as pl
from jax.experimental.pallas import tpu as pltpu
from jax.sharding import PartitionSpec as P

HEAD_DIM = 128
LANES = 128
MESH = pl.DeviceIdType.MESH

epsilon = 1e-06


def exchange(seq_count, tensor_count, slot_cap, table_ref, pairs_ref, x_ref, req, req_smem, stage,
             small_sem, ask_send, ask_recv, seq_send, seq_recv, across_send, across_recv,
             mate_send, mate_recv, relay_send, relay_recv):
    me = lax.axis_index("seq")
    ten = lax.axis_index("tensor")
    mate = ten + 1 - 2 * (ten % 2)
    across = (ten + 2) % tensor_count

    def to(k):
        return (me + k) % seq_count

    def source(k):
        return (me + seq_count - k) % seq_count

    barrier = pltpu.get_barrier_semaphore()

    @pl.loop(1, seq_count)
    def _(k):
        pl.semaphore_signal(barrier, inc=1, device_id=(to(k), ten), device_id_type=MESH)

    pl.semaphore_signal(barrier, inc=1, device_id=(me, mate), device_id_type=MESH)
    pl.semaphore_signal(barrier, inc=1, device_id=(me, across), device_id_type=MESH)
    pl.semaphore_wait(barrier, seq_count + 1)

    def ask(k, landing):
        return pltpu.make_async_remote_copy(
            src_ref=table_ref.at[to(k)], dst_ref=req.at[landing],
            send_sem=ask_send.at[k], recv_sem=ask_recv.at[k],
            device_id=(to(k), ten), device_id_type=MESH,
        )

    def move(k, landing):
        return pltpu.make_async_remote_copy(
            src_ref=stage.at[k], dst_ref=x_ref.at[ten, landing],
            send_sem=seq_send.at[k], recv_sem=seq_recv.at[k],
            device_id=(to(k), ten), device_id_type=MESH,
        )

    def share(part, k, send, recv, other):
        block = x_ref.at[part, source(k)]
        return pltpu.make_async_remote_copy(
            src_ref=block, dst_ref=block, send_sem=send.at[k], recv_sem=recv.at[k],
            device_id=(me, other), device_id_type=MESH,
        )

    def to_across(k, part):
        return share(part, k, across_send, across_recv, across)

    def to_mate(k, part):
        return share(part, k, mate_send, mate_recv, mate)

    def relay(k, part):
        return share(part, k, relay_send, relay_recv, mate)

    @pl.loop(1, seq_count)
    def _(k):
        ask(k, me).start()

    req[me] = table_ref[me]

    @pl.loop(1, seq_count)
    def _(k):
        ask(k, source(k)).wait_recv()

    to_scalar = pltpu.make_async_copy(req, req_smem, small_sem.at[0])
    to_scalar.start()
    to_scalar.wait()

    def fill(k):
        for c in range(slot_cap):
            stage[k, c] = pairs_ref[req_smem[to(k), 0, c]]

    @pl.loop(1, seq_count)
    def _(k):
        fill(k)
        move(k, me).start()

    fill(0)
    own = pltpu.make_async_copy(stage.at[0], x_ref.at[ten, me], small_sem.at[1])
    own.start()
    own.wait()
    to_across(0, ten).start()
    to_mate(0, ten).start()

    def pass_on(k):
        to_across(k, across).wait_recv()
        relay(k, across).start()

    @pl.loop(1, seq_count)
    def _(k):
        move(k, source(k)).wait_recv()
        to_across(k, ten).start()
        to_mate(k, ten).start()
        pass_on(k - 1)

    pass_on(seq_count - 1)

    @pl.loop(1, seq_count)
    def _(k):
        ask(k, me).wait_send()
        move(k, me).wait_send()

    @pl.loop(0, seq_count)
    def _(k):
        to_across(k, ten).wait_send()
        to_mate(k, ten).wait_send()
        relay(k, across).wait_send()
        to_mate(k, mate).wait_recv()
        relay(k, (mate + 2) % tensor_count).wait_recv()


def gathered_states(seq_count, tensor_count, slot_cap, table, pairs):
    feats, toks = pairs.shape[1:]
    dma = pltpu.SemaphoreType.DMA
    return pl.pallas_call(
        functools.partial(exchange, seq_count, tensor_count, slot_cap),
        out_shape=jax.ShapeDtypeStruct((tensor_count, seq_count, slot_cap, feats, toks), jnp.bfloat16),
        in_specs=[pl.BlockSpec(memory_space=pltpu.VMEM)] * 2,
        out_specs=pl.BlockSpec(memory_space=pl.ANY),
        scratch_shapes=[
            pltpu.VMEM((seq_count, 1, LANES), jnp.int32),
            pltpu.SMEM((seq_count, 1, LANES), jnp.int32),
            pltpu.VMEM((seq_count, slot_cap, feats, toks), jnp.bfloat16),
            dma((2,)),
        ] + [dma((seq_count,))] * 10,
        compiler_params=pltpu.CompilerParams(
            collective_id=0, has_side_effects=True, vmem_limit_bytes=32 * 1024 * 1024
        ),
    )(table, pairs)


def attend(enc_width, head_count, slots, first_ref, second_ref, weight_ref, gain_ref, query_ref, out_ref):
    def flat(ref):
        return ref[...].reshape(enc_width, -1)

    as_float = jnp.concatenate([flat(first_ref), flat(second_ref)], axis=1).astype(jnp.float32)
    square_sum = jnp.sum(as_float * as_float, axis=0, keepdims=True)
    inv_rms = lax.rsqrt(square_sum / enc_width + epsilon)
    scaled = (as_float * gain_ref[...]).astype(jnp.bfloat16)
    half = head_count * HEAD_DIM
    kv_sum = jnp.dot(weight_ref[...], scaled, preferred_element_type=jnp.float32)
    keys_values = (kv_sum * inv_rms).astype(jnp.bfloat16)
    for h in range(head_count):
        cols = slice(h * HEAD_DIM, (h + 1) * HEAD_DIM)
        keys = keys_values[h * HEAD_DIM : (h + 1) * HEAD_DIM]
        values = keys_values[half + h * HEAD_DIM : half + (h + 1) * HEAD_DIM]
        scores = jnp.dot(query_ref[:, cols], keys, preferred_element_type=jnp.float32) / math.sqrt(HEAD_DIM)
        expo = jnp.exp(scores - jnp.max(scores, axis=-1, keepdims=True))
        weights = (expo / jnp.sum(expo, axis=-1, keepdims=True)).astype(jnp.bfloat16)
        mixed = lax.dot_general(
            weights, values, (((1,), (1,)), ((), ())), preferred_element_type=jnp.float32
        )
        out_ref[:, cols] = mixed.astype(jnp.bfloat16)


def attended_rows(states, slots, weight, gain, query_win, group_len):
    tensor_count, _, feats, toks = states.shape
    rows, cols = query_win.shape
    enc_width = weight.shape[1]
    head_count = cols // HEAD_DIM
    groups = rows // group_len

    def picked(which):
        return pl.BlockSpec(
            (tensor_count, 1, feats, toks), lambda c, slots: (0, slots[2 * c + which], 0, 0)
        )

    return pl.pallas_call(
        functools.partial(attend, enc_width, head_count),
        grid_spec=pltpu.PrefetchScalarGridSpec(
            num_scalar_prefetch=1,
            grid=(groups,),
            in_specs=[
                picked(0),
                picked(1),
                pl.BlockSpec(weight.shape, lambda c, slots: (0, 0)),
                pl.BlockSpec(gain.shape, lambda c, slots: (0, 0)),
                pl.BlockSpec((group_len, cols), lambda c, slots: (c, 0)),
            ],
            out_specs=pl.BlockSpec((group_len, cols), lambda c, slots: (c, 0)),
        ),
        out_shape=jax.ShapeDtypeStruct((rows, cols), jnp.bfloat16),
        compiler_params=pltpu.CompilerParams(vmem_limit_bytes=40 * 1024 * 1024),
    )(slots, states, states, weight, gain, query_win)


def per_device(queries, db_states, enc_gain, kv_weight, shard_ids, offsets):
    seq_count = lax.axis_size("seq")
    tensor_count = lax.axis_size("tensor")
    group_count = shard_ids.shape[0]
    neigh_count = 2 * group_count
    slot_cap = (neigh_count + seq_count - 1) // seq_count
    group_len = db_states.shape[1]
    enc_width = kv_weight.shape[0]
    edge = group_len - 1
    kept = queries.shape[0] - edge

    back = [(i + 1, i) for i in range(seq_count - 1)]
    forth = [(i, i + 1) for i in range(seq_count - 1)]
    next_rows = lax.ppermute(queries[:group_len], "seq", back)

    shard = shard_ids.reshape(neigh_count)
    offset = offsets.reshape(neigh_count)
    place = jnp.arange(neigh_count, dtype=jnp.int32)
    earlier = (shard[:, None] == shard[None, :]) & (place[None, :] < place[:, None])
    rank = jnp.sum(earlier.astype(jnp.int32), axis=1)
    slots = shard * slot_cap + rank
    owner = jnp.arange(seq_count, dtype=jnp.int32)[:, None, None, None]
    lane = jnp.arange(LANES, dtype=jnp.int32)[None, None, :, None]
    named = (shard[None, None, None, :] == owner) & (rank[None, None, None, :] == lane)
    table = jnp.sum(jnp.where(named, offset[None, None, None, :], 0), axis=-1)

    turned = jnp.transpose(db_states, (0, 2, 1))
    pairs = jnp.concatenate([turned[:-1], turned[1:]], axis=2)
    weight = jnp.transpose(kv_weight, (1, 2, 0)).reshape(-1, enc_width)

    states = gathered_states(seq_count, tensor_count, slot_cap, table, pairs)
    states = states.reshape(tensor_count, seq_count * slot_cap, *states.shape[3:])
    query_win = jnp.concatenate([queries[edge:], next_rows[:edge]], axis=0)
    attended = attended_rows(states, slots, weight, enc_gain.reshape(-1, 1), query_win, group_len)
    previous = lax.ppermute(attended[kept - 1 :], "seq", forth)
    return jnp.concatenate([previous[1:], attended[:kept]], axis=0)


def solution(mesh):
    return jax.shard_map(
        per_device,
        mesh=mesh,
        in_specs=(
            P("seq", "tensor"),
            P("seq", None, "tensor"),
            P(),
            P(None, None, "tensor"),
            P("seq", None),
            P("seq", None),
        ),
        out_specs=P("seq", "tensor"),
        check_vma=False,
    )
```

```python
import functools
import math

import jax
import jax.numpy as jnp
from jax import lax
from jax.experimental import pallas as pl
from jax.experimental.pallas import tpu as pltpu
from jax.sharding import PartitionSpec as P

HEAD_DIM = 128
LANES = 128
ROWS = 256
MESH = pl.DeviceIdType.MESH

epsilon = 1e-06


def exchange(seq_count, tensor_count, slot_cap, table_ref, pairs_ref, weight_ref, gain_ref, kv_ref,
             req, req_smem, stage, x_ref, turned, scaled, kv_held, small_sem, out_sem, ask_send, ask_recv, seq_send, seq_recv, across_send, across_recv,
             mate_send, mate_recv, relay_send, relay_recv):
    me = lax.axis_index("seq")
    ten = lax.axis_index("tensor")
    mate = ten + 1 - 2 * (ten % 2)
    across = (ten + 2) % tensor_count

    def to(k):
        return (me + k) % seq_count

    def source(k):
        return (me + seq_count - k) % seq_count

    barrier = pltpu.get_barrier_semaphore()

    @pl.loop(1, seq_count)
    def _(k):
        pl.semaphore_signal(barrier, inc=1, device_id=(to(k), ten), device_id_type=MESH)

    pl.semaphore_signal(barrier, inc=1, device_id=(me, mate), device_id_type=MESH)
    pl.semaphore_signal(barrier, inc=1, device_id=(me, across), device_id_type=MESH)
    pl.semaphore_wait(barrier, seq_count + 1)

    def ask(k, landing):
        return pltpu.make_async_remote_copy(
            src_ref=table_ref.at[to(k)], dst_ref=req.at[landing],
            send_sem=ask_send.at[k], recv_sem=ask_recv.at[k],
            device_id=(to(k), ten), device_id_type=MESH,
        )

    def move(k, landing):
        return pltpu.make_async_remote_copy(
            src_ref=stage.at[k], dst_ref=x_ref.at[ten, landing],
            send_sem=seq_send.at[k], recv_sem=seq_recv.at[k],
            device_id=(to(k), ten), device_id_type=MESH,
        )

    def share(part, k, send, recv, other):
        block = x_ref.at[part, source(k)]
        return pltpu.make_async_remote_copy(
            src_ref=block, dst_ref=block, send_sem=send.at[k], recv_sem=recv.at[k],
            device_id=(me, other), device_id_type=MESH,
        )

    def to_across(k, part):
        return share(part, k, across_send, across_recv, across)

    def to_mate(k, part):
        return share(part, k, mate_send, mate_recv, mate)

    def relay(k, part):
        return share(part, k, relay_send, relay_recv, mate)

    @pl.loop(1, seq_count)
    def _(k):
        ask(k, me).start()

    req[me] = table_ref[me]
    enc_width, kv_cols = weight_ref.shape

    @pl.loop(0, kv_cols // LANES)
    def _(i):
        cols = pl.ds(pl.multiple_of(i * LANES, LANES), LANES)
        turned[cols, :] = weight_ref[:, cols].T

    @pl.loop(1, seq_count)
    def _(k):
        ask(k, source(k)).wait_recv()

    to_scalar = pltpu.make_async_copy(req, req_smem, small_sem.at[0])
    to_scalar.start()
    to_scalar.wait()

    def fill(k):
        for c in range(slot_cap):
            stage[k, c] = pairs_ref[req_smem[to(k), 0, c]]

    @pl.loop(1, seq_count)
    def _(k):
        fill(k)
        move(k, me).start()

    fill(0)
    own = pltpu.make_async_copy(stage.at[0], x_ref.at[ten, me], small_sem.at[1])
    own.start()
    own.wait()
    to_across(0, ten).start()
    to_mate(0, ten).start()

    def pass_on(k):
        to_across(k, across).wait_recv()
        relay(k, across).start()

    def write_out(k):
        return pltpu.make_async_copy(kv_held.at[k % 2], kv_ref.at[source(k)], out_sem.at[k])

    def project(k):
        to_mate(k, mate).wait_recv()
        relay(k, (mate + 2) % tensor_count).wait_recv()

        @pl.when(k >= 2)
        def _():
            write_out(k - 2).wait()

        inv_rms = []
        for c in range(slot_cap):
            as_float = x_ref[:, source(k), c].reshape(enc_width, LANES).astype(jnp.float32)
            square_sum = jnp.sum(as_float * as_float, axis=0, keepdims=True)
            inv_rms.append(lax.rsqrt(square_sum / enc_width + epsilon))
            scaled[:, c * LANES : (c + 1) * LANES] = (as_float * gain_ref[...]).astype(jnp.bfloat16)

        @pl.loop(0, kv_cols // ROWS)
        def _(i):
            rows = pl.ds(pl.multiple_of(i * ROWS, ROWS), ROWS)
            kv_sum = jnp.dot(turned[rows, :], scaled[...], preferred_element_type=jnp.float32)
            for c in range(slot_cap):
                part = kv_sum[:, c * LANES : (c + 1) * LANES] * inv_rms[c]
                kv_held[k % 2, c, rows, :] = part.astype(jnp.bfloat16)

        write_out(k).start()

    @pl.loop(1, seq_count)
    def _(k):
        move(k, source(k)).wait_recv()
        to_across(k, ten).start()
        to_mate(k, ten).start()
        pass_on(k - 1)

        @pl.when(k >= 2)
        def _():
            project(k - 2)

    pass_on(seq_count - 1)

    @pl.loop(seq_count - 2, seq_count)
    def _(k):
        project(k)

    @pl.loop(1, seq_count)
    def _(k):
        ask(k, me).wait_send()
        move(k, me).wait_send()

    @pl.loop(0, seq_count)
    def _(k):
        to_across(k, ten).wait_send()
        to_mate(k, ten).wait_send()
        relay(k, across).wait_send()

    @pl.loop(seq_count - 2, seq_count)
    def _(k):
        write_out(k).wait()


def gathered_kv(seq_count, tensor_count, slot_cap, table, pairs, weight, gain):
    feats, toks = pairs.shape[1:]
    enc_width, kv_cols = weight.shape
    dma = pltpu.SemaphoreType.DMA
    return pl.pallas_call(
        functools.partial(exchange, seq_count, tensor_count, slot_cap),
        out_shape=jax.ShapeDtypeStruct((seq_count, slot_cap, kv_cols, toks), jnp.bfloat16),
        in_specs=[pl.BlockSpec(memory_space=pltpu.VMEM)] * 4,
        out_specs=pl.BlockSpec(memory_space=pl.ANY),
        scratch_shapes=[
            pltpu.VMEM((seq_count, 1, LANES), jnp.int32),
            pltpu.SMEM((seq_count, 1, LANES), jnp.int32),
            pltpu.VMEM((seq_count, slot_cap, feats, toks), jnp.bfloat16),
            pltpu.VMEM((tensor_count, seq_count, slot_cap, feats, toks), jnp.bfloat16),
            pltpu.VMEM((kv_cols, enc_width), jnp.bfloat16),
            pltpu.VMEM((enc_width, slot_cap * toks), jnp.bfloat16),
            pltpu.VMEM((2, slot_cap, kv_cols, toks), jnp.bfloat16),
            dma((2,)),
        ] + [dma((seq_count,))] * 11,
        compiler_params=pltpu.CompilerParams(
            collective_id=0, has_side_effects=True, vmem_limit_bytes=54 * 1024 * 1024
        ),
    )(table, pairs, weight, gain)


def attend(head_count, slots, first_ref, second_ref, query_ref, out_ref):
    half = head_count * HEAD_DIM
    for h in range(head_count):
        cols = slice(h * HEAD_DIM, (h + 1) * HEAD_DIM)
        late = slice(half + h * HEAD_DIM, half + (h + 1) * HEAD_DIM)
        keys = jnp.concatenate([first_ref[0, cols], second_ref[0, cols]], axis=1)
        values = jnp.concatenate([first_ref[0, late], second_ref[0, late]], axis=1)
        scores = jnp.dot(query_ref[:, cols], keys, preferred_element_type=jnp.float32) / math.sqrt(HEAD_DIM)
        expo = jnp.exp(scores - jnp.max(scores, axis=-1, keepdims=True))
        weights = (expo / jnp.sum(expo, axis=-1, keepdims=True)).astype(jnp.bfloat16)
        mixed = lax.dot_general(
            weights, values, (((1,), (1,)), ((), ())), preferred_element_type=jnp.float32
        )
        out_ref[:, cols] = mixed.astype(jnp.bfloat16)


def attended_rows(kv, slots, query_win, group_len):
    _, kv_cols, toks = kv.shape
    rows, cols = query_win.shape

    def picked(which):
        return pl.BlockSpec((1, kv_cols, toks), lambda c, slots: (slots[2 * c + which], 0, 0))

    return pl.pallas_call(
        functools.partial(attend, cols // HEAD_DIM),
        grid_spec=pltpu.PrefetchScalarGridSpec(
            num_scalar_prefetch=1,
            grid=(rows // group_len,),
            in_specs=[picked(0), picked(1), pl.BlockSpec((group_len, cols), lambda c, slots: (c, 0))],
            out_specs=pl.BlockSpec((group_len, cols), lambda c, slots: (c, 0)),
        ),
        out_shape=jax.ShapeDtypeStruct((rows, cols), jnp.bfloat16),
        compiler_params=pltpu.CompilerParams(vmem_limit_bytes=32 * 1024 * 1024),
    )(slots, kv, kv, query_win)


def per_device(queries, db_states, enc_gain, kv_weight, shard_ids, offsets):
    seq_count = lax.axis_size("seq")
    tensor_count = lax.axis_size("tensor")
    group_count = shard_ids.shape[0]
    neigh_count = 2 * group_count
    slot_cap = (neigh_count + seq_count - 1) // seq_count
    group_len = db_states.shape[1]
    enc_width = kv_weight.shape[0]
    edge = group_len - 1
    kept = queries.shape[0] - edge

    back = [(i + 1, i) for i in range(seq_count - 1)]
    forth = [(i, i + 1) for i in range(seq_count - 1)]
    next_rows = lax.ppermute(queries[:group_len], "seq", back)

    shard = shard_ids.reshape(neigh_count)
    offset = offsets.reshape(neigh_count)
    place = jnp.arange(neigh_count, dtype=jnp.int32)
    earlier = (shard[:, None] == shard[None, :]) & (place[None, :] < place[:, None])
    rank = jnp.sum(earlier.astype(jnp.int32), axis=1)
    slots = shard * slot_cap + rank
    owner = jnp.arange(seq_count, dtype=jnp.int32)[:, None, None, None]
    lane = jnp.arange(LANES, dtype=jnp.int32)[None, None, :, None]
    named = (shard[None, None, None, :] == owner) & (rank[None, None, None, :] == lane)
    table = jnp.sum(jnp.where(named, offset[None, None, None, :], 0), axis=-1)

    turned = jnp.transpose(db_states, (0, 2, 1))
    pairs = jnp.concatenate([turned[:-1], turned[1:]], axis=2)
    weight = kv_weight.reshape(enc_width, -1)

    kv = gathered_kv(seq_count, tensor_count, slot_cap, table, pairs, weight, enc_gain.reshape(-1, 1))
    kv = kv.reshape(seq_count * slot_cap, *kv.shape[2:])
    query_win = jnp.concatenate([queries[edge:], next_rows[:edge]], axis=0)
    attended = attended_rows(kv, slots, query_win, group_len)
    previous = lax.ppermute(attended[kept - 1 :], "seq", forth)
    return jnp.concatenate([previous[1:], attended[:kept]], axis=0)


def solution(mesh):
    return jax.shard_map(
        per_device,
        mesh=mesh,
        in_specs=(
            P("seq", "tensor"),
            P("seq", None, "tensor"),
            P(),
            P(None, None, "tensor"),
            P("seq", None),
            P("seq", None),
        ),
        out_specs=P("seq", "tensor"),
        check_vma=False,
    )
```

```python
import functools
import math

import jax
import jax.numpy as jnp
from jax import lax
from jax.experimental import pallas as pl
from jax.experimental.pallas import tpu as pltpu
from jax.sharding import PartitionSpec as P

HEAD_DIM = 128
LANES = 128
ROWS = 256
FLIGHT = 3
MESH = pl.DeviceIdType.MESH

epsilon = 1e-06


def exchange(seq_count, tensor_count, slot_cap, table_ref, pairs_ref, weight_ref, gain_ref, kv_ref,
             req, req_smem, stage, x_ref, turned, scaled, kv_held, small_sem, out_sem, ask_send, ask_recv, seq_send, seq_recv, across_send, across_recv,
             mate_send, mate_recv, relay_send, relay_recv):
    me = lax.axis_index("seq")
    ten = lax.axis_index("tensor")
    mate = ten + 1 - 2 * (ten % 2)
    across = (ten + 2) % tensor_count

    def to(k):
        far, near = seq_count // 2 + (k - 1) // 2, k // 2
        flip = (k % 2) * far + (1 - k % 2) * near
        bit, other = 1, 0
        while bit < seq_count:
            other = other + ((me // bit + flip // bit) % 2) * bit
            bit *= 2
        return other

    source = to

    barrier = pltpu.get_barrier_semaphore()

    @pl.loop(1, seq_count)
    def _(k):
        pl.semaphore_signal(barrier, inc=1, device_id=(to(k), ten), device_id_type=MESH)

    pl.semaphore_signal(barrier, inc=1, device_id=(me, mate), device_id_type=MESH)
    pl.semaphore_signal(barrier, inc=1, device_id=(me, across), device_id_type=MESH)
    pl.semaphore_wait(barrier, seq_count + 1)

    def ask(k, landing):
        return pltpu.make_async_remote_copy(
            src_ref=table_ref.at[to(k)], dst_ref=req.at[landing],
            send_sem=ask_send.at[k], recv_sem=ask_recv.at[k],
            device_id=(to(k), ten), device_id_type=MESH,
        )

    def move(k, landing):
        return pltpu.make_async_remote_copy(
            src_ref=stage.at[k], dst_ref=x_ref.at[ten, landing],
            send_sem=seq_send.at[k], recv_sem=seq_recv.at[k],
            device_id=(to(k), ten), device_id_type=MESH,
        )

    def share(part, k, send, recv, other):
        block = x_ref.at[part, source(k)]
        return pltpu.make_async_remote_copy(
            src_ref=block, dst_ref=block, send_sem=send.at[k], recv_sem=recv.at[k],
            device_id=(me, other), device_id_type=MESH,
        )

    def to_across(k, part):
        return share(part, k, across_send, across_recv, across)

    def to_mate(k, part):
        return share(part, k, mate_send, mate_recv, mate)

    def relay(k, part):
        return share(part, k, relay_send, relay_recv, mate)

    @pl.loop(1, seq_count)
    def _(k):
        ask(k, me).start()

    req[me] = table_ref[me]

    def fill(k):
        for c in range(slot_cap):
            stage[k, c] = pairs_ref[req_smem[to(k), 0, c]]

    own_ask = pltpu.make_async_copy(table_ref.at[me], req_smem.at[me], small_sem.at[0])
    own_ask.start()
    own_ask.wait()
    fill(0)
    own = pltpu.make_async_copy(stage.at[0], x_ref.at[ten, me], small_sem.at[1])
    own.start()
    own.wait()
    to_across(0, ten).start()
    to_mate(0, ten).start()

    enc_width, kv_cols = weight_ref.shape

    @pl.loop(0, kv_cols // LANES)
    def _(i):
        cols = pl.ds(pl.multiple_of(i * LANES, LANES), LANES)
        turned[cols, :] = weight_ref[:, cols].T

    @pl.loop(1, seq_count)
    def _(k):
        ask(k, source(k)).wait_recv()

    to_scalar = pltpu.make_async_copy(req, req_smem, small_sem.at[0])
    to_scalar.start()
    to_scalar.wait()

    def send(k):
        fill(k)
        move(k, me).start()

    @pl.loop(1, min(FLIGHT + 1, seq_count))
    def _(k):
        send(k)

    def pass_on(k):
        to_across(k, across).wait_recv()
        relay(k, across).start()

    def write_out(k):
        return pltpu.make_async_copy(kv_held.at[k % 2], kv_ref.at[source(k)], out_sem.at[k])

    def project(k):
        to_mate(k, mate).wait_recv()
        relay(k, (mate + 2) % tensor_count).wait_recv()

        @pl.when(k >= 2)
        def _():
            write_out(k - 2).wait()

        inv_rms = []
        for c in range(slot_cap):
            as_float = x_ref[:, source(k), c].reshape(enc_width, LANES).astype(jnp.float32)
            square_sum = jnp.sum(as_float * as_float, axis=0, keepdims=True)
            inv_rms.append(lax.rsqrt(square_sum / enc_width + epsilon))
            scaled[:, c * LANES : (c + 1) * LANES] = (as_float * gain_ref[...]).astype(jnp.bfloat16)

        @pl.loop(0, kv_cols // ROWS)
        def _(i):
            rows = pl.ds(pl.multiple_of(i * ROWS, ROWS), ROWS)
            kv_sum = jnp.dot(turned[rows, :], scaled[...], preferred_element_type=jnp.float32)
            for c in range(slot_cap):
                part = kv_sum[:, c * LANES : (c + 1) * LANES] * inv_rms[c]
                kv_held[k % 2, c, rows, :] = part.astype(jnp.bfloat16)

        write_out(k).start()

    @pl.loop(1, seq_count)
    def _(k):
        move(k, me).wait_send()

        @pl.when(k + FLIGHT < seq_count)
        def _():
            send(k + FLIGHT)

        move(k, source(k)).wait_recv()
        to_across(k, ten).start()
        to_mate(k, ten).start()
        pass_on(k - 1)

        @pl.when(k >= 2)
        def _():
            project(k - 2)

    pass_on(seq_count - 1)

    @pl.loop(seq_count - 2, seq_count)
    def _(k):
        project(k)

    @pl.loop(1, seq_count)
    def _(k):
        ask(k, me).wait_send()

    @pl.loop(0, seq_count)
    def _(k):
        to_across(k, ten).wait_send()
        to_mate(k, ten).wait_send()
        relay(k, across).wait_send()

    @pl.loop(seq_count - 2, seq_count)
    def _(k):
        write_out(k).wait()


def gathered_kv(seq_count, tensor_count, slot_cap, table, pairs, weight, gain):
    feats, toks = pairs.shape[1:]
    enc_width, kv_cols = weight.shape
    dma = pltpu.SemaphoreType.DMA
    return pl.pallas_call(
        functools.partial(exchange, seq_count, tensor_count, slot_cap),
        out_shape=jax.ShapeDtypeStruct((seq_count, slot_cap, kv_cols, toks), jnp.bfloat16),
        in_specs=[pl.BlockSpec(memory_space=pltpu.VMEM)] * 4,
        out_specs=pl.BlockSpec(memory_space=pl.ANY),
        scratch_shapes=[
            pltpu.VMEM((seq_count, 1, LANES), jnp.int32),
            pltpu.SMEM((seq_count, 1, LANES), jnp.int32),
            pltpu.VMEM((seq_count, slot_cap, feats, toks), jnp.bfloat16),
            pltpu.VMEM((tensor_count, seq_count, slot_cap, feats, toks), jnp.bfloat16),
            pltpu.VMEM((kv_cols, enc_width), jnp.bfloat16),
            pltpu.VMEM((enc_width, slot_cap * toks), jnp.bfloat16),
            pltpu.VMEM((2, slot_cap, kv_cols, toks), jnp.bfloat16),
            dma((2,)),
        ] + [dma((seq_count,))] * 11,
        compiler_params=pltpu.CompilerParams(
            collective_id=0, has_side_effects=True, vmem_limit_bytes=54 * 1024 * 1024
        ),
    )(table, pairs, weight, gain)


def attend(head_count, slots, first_ref, second_ref, query_ref, out_ref):
    half = head_count * HEAD_DIM
    for h in range(head_count):
        cols = slice(h * HEAD_DIM, (h + 1) * HEAD_DIM)
        late = slice(half + h * HEAD_DIM, half + (h + 1) * HEAD_DIM)
        keys = jnp.concatenate([first_ref[0, cols], second_ref[0, cols]], axis=1)
        values = jnp.concatenate([first_ref[0, late], second_ref[0, late]], axis=1)
        scores = jnp.dot(query_ref[:, cols], keys, preferred_element_type=jnp.float32)
        lowered = scores - jnp.max(scores, axis=-1, keepdims=True)
        expo = jnp.exp(lowered * (1.0 / math.sqrt(HEAD_DIM)))
        weights = (expo * (1.0 / jnp.sum(expo, axis=-1, keepdims=True))).astype(jnp.bfloat16)
        mixed = lax.dot_general(
            weights, values, (((1,), (1,)), ((), ())), preferred_element_type=jnp.float32
        )
        out_ref[:, cols] = mixed.astype(jnp.bfloat16)


def attended_rows(kv, slots, query_win, group_len):
    _, kv_cols, toks = kv.shape
    rows, cols = query_win.shape

    def picked(which):
        return pl.BlockSpec((1, kv_cols, toks), lambda c, slots: (slots[2 * c + which], 0, 0))

    return pl.pallas_call(
        functools.partial(attend, cols // HEAD_DIM),
        grid_spec=pltpu.PrefetchScalarGridSpec(
            num_scalar_prefetch=1,
            grid=(rows // group_len,),
            in_specs=[picked(0), picked(1), pl.BlockSpec((group_len, cols), lambda c, slots: (c, 0))],
            out_specs=pl.BlockSpec((group_len, cols), lambda c, slots: (c, 0)),
        ),
        out_shape=jax.ShapeDtypeStruct((rows, cols), jnp.bfloat16),
        compiler_params=pltpu.CompilerParams(vmem_limit_bytes=60 * 1024 * 1024),
        cost_estimate=pl.CostEstimate(
            flops=16 * rows * group_len * cols, bytes_accessed=2 * rows * 16 * cols, transcendentals=0
        ),
    )(slots, kv, kv, query_win)


def per_device(queries, db_states, enc_gain, kv_weight, shard_ids, offsets):
    seq_count = lax.axis_size("seq")
    tensor_count = lax.axis_size("tensor")
    group_count = shard_ids.shape[0]
    neigh_count = 2 * group_count
    slot_cap = (neigh_count + seq_count - 1) // seq_count
    group_len = db_states.shape[1]
    enc_width = kv_weight.shape[0]
    edge = group_len - 1
    kept = queries.shape[0] - edge

    back = [(i + 1, i) for i in range(seq_count - 1)]
    forth = [(i, i + 1) for i in range(seq_count - 1)]
    next_rows = lax.ppermute(queries[:group_len], "seq", back)

    shard = shard_ids.reshape(neigh_count)
    offset = offsets.reshape(neigh_count)
    place = jnp.arange(neigh_count, dtype=jnp.int32)
    earlier = (shard[:, None] == shard[None, :]) & (place[None, :] < place[:, None])
    rank = jnp.sum(earlier.astype(jnp.int32), axis=1)
    slots = shard * slot_cap + rank
    owner = jnp.arange(seq_count, dtype=jnp.int32)[:, None, None, None]
    lane = jnp.arange(LANES, dtype=jnp.int32)[None, None, :, None]
    named = (shard[None, None, None, :] == owner) & (rank[None, None, None, :] == lane)
    table = jnp.sum(jnp.where(named, offset[None, None, None, :], 0), axis=-1)

    turned = jnp.transpose(db_states, (0, 2, 1))
    pairs = jnp.concatenate([turned[:-1], turned[1:]], axis=2)
    weight = kv_weight.reshape(enc_width, -1)

    kv = gathered_kv(seq_count, tensor_count, slot_cap, table, pairs, weight, enc_gain.reshape(-1, 1))
    kv = kv.reshape(seq_count * slot_cap, *kv.shape[2:])
    last_win = jnp.concatenate([queries[kept + edge - 1 :], next_rows[:edge]], axis=0)
    last = attended_rows(kv, slots[-2:], last_win, group_len)
    previous = lax.ppermute(last, "seq", forth)
    rest = attended_rows(kv, slots[:-2], queries[edge : kept + edge - 1], group_len)
    return jnp.concatenate([previous[1:], rest, last[:1]], axis=0)


def solution(mesh):
    return jax.shard_map(
        per_device,
        mesh=mesh,
        in_specs=(
            P("seq", "tensor"),
            P("seq", None, "tensor"),
            P(),
            P(None, None, "tensor"),
            P("seq", None),
            P("seq", None),
        ),
        out_specs=P("seq", "tensor"),
        check_vma=False,
    )
```

```python
import functools
import math

import jax
import jax.numpy as jnp
from jax import lax
from jax.experimental import pallas as pl
from jax.experimental.pallas import tpu as pltpu
from jax.sharding import PartitionSpec as P

HEAD_DIM = 128
LANES = 128
ROWS = 256
MESH = pl.DeviceIdType.MESH

epsilon = 1e-06


def exchange(seq_count, tensor_count, slot_cap, table_ref, pairs_ref, weight_ref, gain_ref, kv_ref,
             req, req_smem, stage, x_ref, turned, scaled, kv_held, small_sem, out_sem, ask_send, ask_recv, seq_send, seq_recv, across_send, across_recv,
             mate_send, mate_recv, relay_send, relay_recv):
    me = lax.axis_index("seq")
    ten = lax.axis_index("tensor")
    mate = ten + 1 - 2 * (ten % 2)
    across = (ten + 2) % tensor_count

    def to(k):
        return (me + k) % seq_count

    def source(k):
        return (me + seq_count - k) % seq_count

    barrier = pltpu.get_barrier_semaphore()

    @pl.loop(1, seq_count)
    def _(k):
        pl.semaphore_signal(barrier, inc=1, device_id=(to(k), ten), device_id_type=MESH)

    pl.semaphore_signal(barrier, inc=1, device_id=(me, mate), device_id_type=MESH)
    pl.semaphore_signal(barrier, inc=1, device_id=(me, across), device_id_type=MESH)
    pl.semaphore_wait(barrier, seq_count + 1)

    def ask(k, landing):
        return pltpu.make_async_remote_copy(
            src_ref=table_ref.at[to(k)], dst_ref=req.at[landing],
            send_sem=ask_send.at[k], recv_sem=ask_recv.at[k],
            device_id=(to(k), ten), device_id_type=MESH,
        )

    def move(k, landing):
        return pltpu.make_async_remote_copy(
            src_ref=stage.at[k], dst_ref=x_ref.at[ten, landing],
            send_sem=seq_send.at[k], recv_sem=seq_recv.at[k],
            device_id=(to(k), ten), device_id_type=MESH,
        )

    def share(part, k, send, recv, other):
        block = x_ref.at[part, source(k)]
        return pltpu.make_async_remote_copy(
            src_ref=block, dst_ref=block, send_sem=send.at[k], recv_sem=recv.at[k],
            device_id=(me, other), device_id_type=MESH,
        )

    def to_across(k, part):
        return share(part, k, across_send, across_recv, across)

    def to_mate(k, part):
        return share(part, k, mate_send, mate_recv, mate)

    def relay(k, part):
        return share(part, k, relay_send, relay_recv, mate)

    @pl.loop(1, seq_count)
    def _(k):
        ask(k, me).start()

    req[me] = table_ref[me]
    enc_width, kv_cols = weight_ref.shape

    @pl.loop(0, kv_cols // LANES)
    def _(i):
        cols = pl.ds(pl.multiple_of(i * LANES, LANES), LANES)
        turned[cols, :] = weight_ref[:, cols].T

    @pl.loop(1, seq_count)
    def _(k):
        ask(k, source(k)).wait_recv()

    to_scalar = pltpu.make_async_copy(req, req_smem, small_sem.at[0])
    to_scalar.start()
    to_scalar.wait()

    def fill(k):
        for c in range(slot_cap):
            stage[k, c] = pairs_ref[req_smem[to(k), 0, c]]

    @pl.loop(1, seq_count)
    def _(k):
        fill(k)
        move(k, me).start()

    fill(0)
    own = pltpu.make_async_copy(stage.at[0], x_ref.at[ten, me], small_sem.at[1])
    own.start()
    own.wait()
    to_across(0, ten).start()
    to_mate(0, ten).start()

    def pass_on(k):
        to_across(k, across).wait_recv()
        relay(k, across).start()

    def write_out(k):
        return pltpu.make_async_copy(kv_held.at[k % 2], kv_ref.at[source(k)], out_sem.at[k])

    def project(k):
        to_mate(k, mate).wait_recv()
        relay(k, (mate + 2) % tensor_count).wait_recv()

        @pl.when(k >= 2)
        def _():
            write_out(k - 2).wait()

        inv_rms = []
        for c in range(slot_cap):
            as_float = x_ref[:, source(k), c].reshape(enc_width, LANES).astype(jnp.float32)
            square_sum = jnp.sum(as_float * as_float, axis=0, keepdims=True)
            inv_rms.append(lax.rsqrt(square_sum / enc_width + epsilon))
            scaled[:, c * LANES : (c + 1) * LANES] = (as_float * gain_ref[...]).astype(jnp.bfloat16)

        @pl.loop(0, kv_cols // ROWS)
        def _(i):
            rows = pl.ds(pl.multiple_of(i * ROWS, ROWS), ROWS)
            kv_sum = jnp.dot(turned[rows, :], scaled[...], preferred_element_type=jnp.float32)
            for c in range(slot_cap):
                part = kv_sum[:, c * LANES : (c + 1) * LANES] * inv_rms[c]
                kv_held[k % 2, c, rows, :] = part.astype(jnp.bfloat16)

        write_out(k).start()

    @pl.loop(1, seq_count)
    def _(k):
        move(k, source(k)).wait_recv()
        to_across(k, ten).start()
        to_mate(k, ten).start()
        pass_on(k - 1)

        @pl.when(k >= 2)
        def _():
            project(k - 2)

    pass_on(seq_count - 1)

    @pl.loop(seq_count - 2, seq_count)
    def _(k):
        project(k)

    @pl.loop(1, seq_count)
    def _(k):
        ask(k, me).wait_send()
        move(k, me).wait_send()

    @pl.loop(0, seq_count)
    def _(k):
        to_across(k, ten).wait_send()
        to_mate(k, ten).wait_send()
        relay(k, across).wait_send()

    @pl.loop(seq_count - 2, seq_count)
    def _(k):
        write_out(k).wait()


def gathered_kv(seq_count, tensor_count, slot_cap, table, pairs, weight, gain):
    feats, toks = pairs.shape[1:]
    enc_width, kv_cols = weight.shape
    dma = pltpu.SemaphoreType.DMA
    return pl.pallas_call(
        functools.partial(exchange, seq_count, tensor_count, slot_cap),
        out_shape=jax.ShapeDtypeStruct((seq_count, slot_cap, kv_cols, toks), jnp.bfloat16),
        in_specs=[pl.BlockSpec(memory_space=pltpu.VMEM)] * 4,
        out_specs=pl.BlockSpec(memory_space=pl.ANY),
        scratch_shapes=[
            pltpu.VMEM((seq_count, 1, LANES), jnp.int32),
            pltpu.SMEM((seq_count, 1, LANES), jnp.int32),
            pltpu.VMEM((seq_count, slot_cap, feats, toks), jnp.bfloat16),
            pltpu.VMEM((tensor_count, seq_count, slot_cap, feats, toks), jnp.bfloat16),
            pltpu.VMEM((kv_cols, enc_width), jnp.bfloat16),
            pltpu.VMEM((enc_width, slot_cap * toks), jnp.bfloat16),
            pltpu.VMEM((2, slot_cap, kv_cols, toks), jnp.bfloat16),
            dma((2,)),
        ] + [dma((seq_count,))] * 11,
        compiler_params=pltpu.CompilerParams(
            collective_id=0, has_side_effects=True, vmem_limit_bytes=54 * 1024 * 1024
        ),
    )(table, pairs, weight, gain)


def attend(head_count, group_len, slots, *refs):
    *kv_refs, query_ref, out_ref = refs
    half = head_count * HEAD_DIM
    for g in range(len(kv_refs) // 2):
        pair = kv_refs[2 * g : 2 * g + 2]
        rows = slice(g * group_len, (g + 1) * group_len)
        for h in range(head_count):
            cols = slice(h * HEAD_DIM, (h + 1) * HEAD_DIM)
            late = slice(half + h * HEAD_DIM, half + (h + 1) * HEAD_DIM)
            keys = jnp.concatenate([ref[0, cols] for ref in pair], axis=1)
            values = jnp.concatenate([ref[0, late] for ref in pair], axis=1)
            scores = jnp.dot(query_ref[rows, cols], keys, preferred_element_type=jnp.float32)
            lowered = scores - jnp.max(scores, axis=-1, keepdims=True)
            expo = jnp.exp(lowered * (1.0 / math.sqrt(HEAD_DIM)))
            weights = (expo * (1.0 / jnp.sum(expo, axis=-1, keepdims=True))).astype(jnp.bfloat16)
            mixed = lax.dot_general(
                weights, values, (((1,), (1,)), ((), ())), preferred_element_type=jnp.float32
            )
            out_ref[rows, cols] = mixed.astype(jnp.bfloat16)


def attended_rows(kv, slots, query_win, group_len):
    _, kv_cols, toks = kv.shape
    rows, cols = query_win.shape
    at_once = 2 if (rows // group_len) % 2 == 0 else 1
    picks = 2 * at_once

    def picked(which):
        return pl.BlockSpec((1, kv_cols, toks), lambda c, slots: (slots[picks * c + which], 0, 0))

    tile = pl.BlockSpec((at_once * group_len, cols), lambda c, slots: (c, 0))
    return pl.pallas_call(
        functools.partial(attend, cols // HEAD_DIM, group_len),
        grid_spec=pltpu.PrefetchScalarGridSpec(
            num_scalar_prefetch=1,
            grid=(rows // (at_once * group_len),),
            in_specs=[picked(i) for i in range(picks)] + [tile],
            out_specs=tile,
        ),
        out_shape=jax.ShapeDtypeStruct((rows, cols), jnp.bfloat16),
        compiler_params=pltpu.CompilerParams(vmem_limit_bytes=60 * 1024 * 1024),
    )(slots, *[kv] * picks, query_win)


def per_device(queries, db_states, enc_gain, kv_weight, shard_ids, offsets):
    seq_count = lax.axis_size("seq")
    tensor_count = lax.axis_size("tensor")
    group_count = shard_ids.shape[0]
    neigh_count = 2 * group_count
    slot_cap = (neigh_count + seq_count - 1) // seq_count
    group_len = db_states.shape[1]
    enc_width = kv_weight.shape[0]
    edge = group_len - 1
    kept = queries.shape[0] - edge

    back = [(i + 1, i) for i in range(seq_count - 1)]
    forth = [(i, i + 1) for i in range(seq_count - 1)]
    next_rows = lax.ppermute(queries[:group_len], "seq", back)

    shard = shard_ids.reshape(neigh_count)
    offset = offsets.reshape(neigh_count)
    place = jnp.arange(neigh_count, dtype=jnp.int32)
    earlier = (shard[:, None] == shard[None, :]) & (place[None, :] < place[:, None])
    rank = jnp.sum(earlier.astype(jnp.int32), axis=1)
    slots = shard * slot_cap + rank
    owner = jnp.arange(seq_count, dtype=jnp.int32)[:, None, None, None]
    lane = jnp.arange(LANES, dtype=jnp.int32)[None, None, :, None]
    named = (shard[None, None, None, :] == owner) & (rank[None, None, None, :] == lane)
    table = jnp.sum(jnp.where(named, offset[None, None, None, :], 0), axis=-1)

    turned = jnp.transpose(db_states, (0, 2, 1))
    pairs = jnp.concatenate([turned[:-1], turned[1:]], axis=2)
    weight = kv_weight.reshape(enc_width, -1)

    kv = gathered_kv(seq_count, tensor_count, slot_cap, table, pairs, weight, enc_gain.reshape(-1, 1))
    kv = kv.reshape(seq_count * slot_cap, *kv.shape[2:])
    query_win = jnp.concatenate([queries[edge:], next_rows[:edge]], axis=0)
    attended = attended_rows(kv, slots, query_win, group_len)
    previous = lax.ppermute(attended[kept - 1 :], "seq", forth)
    return jnp.concatenate([previous[1:], attended[:kept]], axis=0)


def solution(mesh):
    return jax.shard_map(
        per_device,
        mesh=mesh,
        in_specs=(
            P("seq", "tensor"),
            P("seq", None, "tensor"),
            P(),
            P(None, None, "tensor"),
            P("seq", None),
            P("seq", None),
        ),
        out_specs=P("seq", "tensor"),
        check_vma=False,
    )
```

```python
import functools
import math

import jax
import jax.numpy as jnp
from jax import lax
from jax.experimental import pallas as pl
from jax.experimental.pallas import tpu as pltpu
from jax.sharding import PartitionSpec as P

HEAD_DIM = 128
LANES = 128
ROWS = 256
MESH = pl.DeviceIdType.MESH

epsilon = 1e-06


def exchange(seq_count, tensor_count, slot_cap, table_ref, pairs_ref, weight_ref, gain_ref, kv_ref,
             req, req_smem, stage, x_ref, turned, scaled, kv_held, small_sem, out_sem, ask_send, ask_recv, seq_send, seq_recv, across_send, across_recv,
             mate_send, mate_recv, relay_send, relay_recv):
    me = lax.axis_index("seq")
    ten = lax.axis_index("tensor")
    mate = ten + 1 - 2 * (ten % 2)
    across = (ten + 2) % tensor_count

    def to(k):
        return (me + k) % seq_count

    def source(k):
        return (me + seq_count - k) % seq_count

    barrier = pltpu.get_barrier_semaphore()

    @pl.loop(1, seq_count)
    def _(k):
        pl.semaphore_signal(barrier, inc=1, device_id=(to(k), ten), device_id_type=MESH)

    pl.semaphore_signal(barrier, inc=1, device_id=(me, mate), device_id_type=MESH)
    pl.semaphore_signal(barrier, inc=1, device_id=(me, across), device_id_type=MESH)
    pl.semaphore_wait(barrier, seq_count + 1)

    def ask(k, landing):
        return pltpu.make_async_remote_copy(
            src_ref=table_ref.at[to(k)], dst_ref=req.at[landing],
            send_sem=ask_send.at[k], recv_sem=ask_recv.at[k],
            device_id=(to(k), ten), device_id_type=MESH,
        )

    def move(k, landing):
        return pltpu.make_async_remote_copy(
            src_ref=stage.at[k], dst_ref=x_ref.at[ten, landing],
            send_sem=seq_send.at[k], recv_sem=seq_recv.at[k],
            device_id=(to(k), ten), device_id_type=MESH,
        )

    def share(part, k, send, recv, other):
        block = x_ref.at[part, source(k)]
        return pltpu.make_async_remote_copy(
            src_ref=block, dst_ref=block, send_sem=send.at[k], recv_sem=recv.at[k],
            device_id=(me, other), device_id_type=MESH,
        )

    def to_across(k, part):
        return share(part, k, across_send, across_recv, across)

    def to_mate(k, part):
        return share(part, k, mate_send, mate_recv, mate)

    def relay(k, part):
        return share(part, k, relay_send, relay_recv, mate)

    @pl.loop(1, seq_count)
    def _(k):
        ask(k, me).start()

    req[me] = table_ref[me]
    enc_width, kv_cols = weight_ref.shape

    @pl.loop(0, kv_cols // LANES)
    def _(i):
        cols = pl.ds(pl.multiple_of(i * LANES, LANES), LANES)
        turned[cols, :] = weight_ref[:, cols].T

    @pl.loop(1, seq_count)
    def _(k):
        ask(k, source(k)).wait_recv()

    to_scalar = pltpu.make_async_copy(req, req_smem, small_sem.at[0])
    to_scalar.start()
    to_scalar.wait()

    def fill(k):
        for c in range(slot_cap):
            stage[k, c] = pairs_ref[req_smem[to(k), 0, c]]

    @pl.loop(1, seq_count)
    def _(k):
        fill(k)
        move(k, me).start()

    fill(0)
    own = pltpu.make_async_copy(stage.at[0], x_ref.at[ten, me], small_sem.at[1])
    own.start()
    own.wait()
    to_across(0, ten).start()
    to_mate(0, ten).start()

    def pass_on(k):
        to_across(k, across).wait_recv()
        relay(k, across).start()

    def write_out(k):
        return pltpu.make_async_copy(kv_held.at[k % 2], kv_ref.at[source(k)], out_sem.at[k])

    def project(k):
        to_mate(k, mate).wait_recv()
        relay(k, (mate + 2) % tensor_count).wait_recv()

        @pl.when(k >= 2)
        def _():
            write_out(k - 2).wait()

        inv_rms = []
        for c in range(slot_cap):
            as_float = x_ref[:, source(k), c].reshape(enc_width, LANES).astype(jnp.float32)
            square_sum = jnp.sum(as_float * as_float, axis=0, keepdims=True)
            inv_rms.append(lax.rsqrt(square_sum / enc_width + epsilon))
            scaled[:, c * LANES : (c + 1) * LANES] = (as_float * gain_ref[...]).astype(jnp.bfloat16)

        @pl.loop(0, kv_cols // ROWS)
        def _(i):
            rows = pl.ds(pl.multiple_of(i * ROWS, ROWS), ROWS)
            kv_sum = jnp.dot(turned[rows, :], scaled[...], preferred_element_type=jnp.float32)
            for c in range(slot_cap):
                part = kv_sum[:, c * LANES : (c + 1) * LANES] * inv_rms[c]
                kv_held[k % 2, c, rows, :] = part.astype(jnp.bfloat16)

        write_out(k).start()

    @pl.loop(1, seq_count)
    def _(k):
        move(k, source(k)).wait_recv()
        to_across(k, ten).start()
        to_mate(k, ten).start()
        pass_on(k - 1)

        @pl.when(k >= 2)
        def _():
            project(k - 2)

    pass_on(seq_count - 1)

    @pl.loop(seq_count - 2, seq_count)
    def _(k):
        project(k)

    @pl.loop(1, seq_count)
    def _(k):
        ask(k, me).wait_send()
        move(k, me).wait_send()

    @pl.loop(0, seq_count)
    def _(k):
        to_across(k, ten).wait_send()
        to_mate(k, ten).wait_send()
        relay(k, across).wait_send()

    @pl.loop(seq_count - 2, seq_count)
    def _(k):
        write_out(k).wait()


def gathered_kv(seq_count, tensor_count, slot_cap, table, pairs, weight, gain):
    feats, toks = pairs.shape[1:]
    enc_width, kv_cols = weight.shape
    dma = pltpu.SemaphoreType.DMA
    states = 2 * (tensor_count + 1) * seq_count * slot_cap * feats * toks
    need = states + 6 * enc_width * kv_cols + 4 * slot_cap * kv_cols * toks
    return pl.pallas_call(
        functools.partial(exchange, seq_count, tensor_count, slot_cap),
        out_shape=jax.ShapeDtypeStruct((seq_count, slot_cap, kv_cols, toks), jnp.bfloat16),
        in_specs=[pl.BlockSpec(memory_space=pltpu.VMEM)] * 4,
        out_specs=pl.BlockSpec(memory_space=pl.ANY),
        scratch_shapes=[
            pltpu.VMEM((seq_count, 1, LANES), jnp.int32),
            pltpu.SMEM((seq_count, 1, LANES), jnp.int32),
            pltpu.VMEM((seq_count, slot_cap, feats, toks), jnp.bfloat16),
            pltpu.VMEM((tensor_count, seq_count, slot_cap, feats, toks), jnp.bfloat16),
            pltpu.VMEM((kv_cols, enc_width), jnp.bfloat16),
            pltpu.VMEM((enc_width, slot_cap * toks), jnp.bfloat16),
            pltpu.VMEM((2, slot_cap, kv_cols, toks), jnp.bfloat16),
            dma((2,)),
        ] + [dma((seq_count,))] * 11,
        compiler_params=pltpu.CompilerParams(
            collective_id=0, has_side_effects=True, vmem_limit_bytes=need + 10 * 1024 * 1024
        ),
    )(table, pairs, weight, gain)


def attend(head_count, group_len, slots, *refs):
    *kv_refs, query_ref, out_ref = refs
    half = head_count * HEAD_DIM
    for g in range(len(kv_refs) // 2):
        pair = kv_refs[2 * g : 2 * g + 2]
        rows = slice(g * group_len, (g + 1) * group_len)
        for h in range(head_count):
            cols = slice(h * HEAD_DIM, (h + 1) * HEAD_DIM)
            late = slice(half + h * HEAD_DIM, half + (h + 1) * HEAD_DIM)
            keys = jnp.concatenate([ref[0, cols] for ref in pair], axis=1)
            values = jnp.concatenate([ref[0, late] for ref in pair], axis=1)
            scores = jnp.dot(query_ref[rows, cols], keys, preferred_element_type=jnp.float32)
            lowered = scores - jnp.max(scores, axis=-1, keepdims=True)
            expo = jnp.exp(lowered * (1.0 / math.sqrt(HEAD_DIM)))
            weights = (expo * (1.0 / jnp.sum(expo, axis=-1, keepdims=True))).astype(jnp.bfloat16)
            mixed = lax.dot_general(
                weights, values, (((1,), (1,)), ((), ())), preferred_element_type=jnp.float32
            )
            out_ref[rows, cols] = mixed.astype(jnp.bfloat16)


def attended_rows(kv, slots, query_win, group_len):
    _, kv_cols, toks = kv.shape
    rows, cols = query_win.shape
    at_once = 2 if (rows // group_len) % 2 == 0 else 1
    picks = 2 * at_once

    def picked(which):
        return pl.BlockSpec((1, kv_cols, toks), lambda c, slots: (slots[picks * c + which], 0, 0))

    tile = pl.BlockSpec((at_once * group_len, cols), lambda c, slots: (c, 0))
    return pl.pallas_call(
        functools.partial(attend, cols // HEAD_DIM, group_len),
        grid_spec=pltpu.PrefetchScalarGridSpec(
            num_scalar_prefetch=1,
            grid=(rows // (at_once * group_len),),
            in_specs=[picked(i) for i in range(picks)] + [tile],
            out_specs=tile,
        ),
        out_shape=jax.ShapeDtypeStruct((rows, cols), jnp.bfloat16),
        compiler_params=pltpu.CompilerParams(vmem_limit_bytes=24 * 1024 * 1024),
    )(slots, *[kv] * picks, query_win)


def per_device(queries, db_states, enc_gain, kv_weight, shard_ids, offsets):
    seq_count = lax.axis_size("seq")
    tensor_count = lax.axis_size("tensor")
    group_count = shard_ids.shape[0]
    neigh_count = 2 * group_count
    slot_cap = (neigh_count + seq_count - 1) // seq_count
    group_len = db_states.shape[1]
    enc_width = kv_weight.shape[0]
    edge = group_len - 1
    kept = queries.shape[0] - edge

    back = [(i + 1, i) for i in range(seq_count - 1)]
    forth = [(i, i + 1) for i in range(seq_count - 1)]
    next_rows = lax.ppermute(queries[:group_len], "seq", back)

    shard = shard_ids.reshape(neigh_count)
    offset = offsets.reshape(neigh_count)
    place = jnp.arange(neigh_count, dtype=jnp.int32)
    earlier = (shard[:, None] == shard[None, :]) & (place[None, :] < place[:, None])
    rank = jnp.sum(earlier.astype(jnp.int32), axis=1)
    slots = shard * slot_cap + rank
    owner = jnp.arange(seq_count, dtype=jnp.int32)[:, None, None, None]
    lane = jnp.arange(LANES, dtype=jnp.int32)[None, None, :, None]
    named = (shard[None, None, None, :] == owner) & (rank[None, None, None, :] == lane)
    table = jnp.sum(jnp.where(named, offset[None, None, None, :], 0), axis=-1)

    turned = jnp.transpose(db_states, (0, 2, 1))
    pairs = jnp.concatenate([turned[:-1], turned[1:]], axis=2)
    weight = kv_weight.reshape(enc_width, -1)

    kv = gathered_kv(seq_count, tensor_count, slot_cap, table, pairs, weight, enc_gain.reshape(-1, 1))
    kv = kv.reshape(seq_count * slot_cap, *kv.shape[2:])
    query_win = jnp.concatenate([queries[edge:], next_rows[:edge]], axis=0)
    attended = attended_rows(kv, slots, query_win, group_len)
    previous = lax.ppermute(attended[kept - 1 :], "seq", forth)
    return jnp.concatenate([previous[1:], attended[:kept]], axis=0)


def solution(mesh):
    return jax.shard_map(
        per_device,
        mesh=mesh,
        in_specs=(
            P("seq", "tensor"),
            P("seq", None, "tensor"),
            P(),
            P(None, None, "tensor"),
            P("seq", None),
            P("seq", None),
        ),
        out_specs=P("seq", "tensor"),
        check_vma=False,
    )
```
